128 devices in a mesh: fsdp: 32 (over z, x, core), rep: 4 (over y).
Axes of the slice: x: 4, y: 4, z: 4, core: 2. Of those that a mesh axis runs over, the one named last changes fastest.
Arguments:
- gradient: float32 [4, 2048, 16384], P('rep', 'fsdp'), may hold values from -0.6 to 0.6
- block_owner_table: int32 [4, 32], replicated, may hold values from 0 to 127, as said below
- statistics: float32 [128, 4, 2, 512, 512], P(('fsdp', 'rep')), as said below
- inverse_fourth_roots: bfloat16 [128, 4, 2, 512, 512], P(('fsdp', 'rep')), as said below
Outputs:
- direction: float32 [2048, 16384], P('fsdp', 'rep')
- new_statistics: float32 [128, 4, 2, 512, 512], P(('fsdp', 'rep'))
The draws below stay inside these ranges and needn't reach their ends.
Inputs may be any that keep to these rules, and one draw needn't show every extreme that they name: `block_owner_table`: the 32 blocks of one row block have 32 different owners. A device owns at most 4 blocks, and some device owns exactly 4. Slot s of device o holds the statistics of the block of o that is s-th in increasing row block; slots beyond o's count of blocks are never read. Each matrix is symmetric. `inverse_fourth_roots`: laid out as statistics; slots beyond a device's count of blocks are never read. Each matrix is symmetric.
All inputs are finite; a program needn't handle non-finite values.
Results may differ from the reference program's by a relative error of at most 0.0003.
Values sent between devices are 32-bit elements; how exact they have to be, the bound alone decides.
A program may use at most 192 MiB of HBM per device.

```python
import math
import jax
import jax.numpy as jnp
from jax import lax

B = 512
ROWS = 2048
COLS = 16384
RB = 4
CB = 32
SLOTS = 4
N_FSDP = 32
N_REP = 4


def assemble(diagonal, noise):
    sym_part = (noise + jnp.swapaxes(noise, -1, -2)) * (0.7071 * 0.27 / math.sqrt(B))
    identity = jnp.eye(B, dtype=jnp.float32)
    sqrt_diag = jnp.sqrt(diagonal)
    return sqrt_diag[..., :, None] * (identity + sym_part * (1.0 - identity)) * sqrt_diag[..., None, :]


def draw_block_owner_table(key, part):
    key = jax.random.fold_in(key, 11)
    key_busy, key_count, key_rows = jax.random.split(key, 3)
    worker_count = N_FSDP * N_REP
    order = jax.random.permutation(key_busy, worker_count)
    priority_order = jnp.argsort(order)
    loaded_count = jax.random.randint(key_count, (), 1, CB // 4 + 1)
    extra_credit = jnp.where(priority_order < loaded_count, 2 * worker_count, 0)

    def one_row(row_key):
        key_priority, key_mix = jax.random.split(row_key)
        owner_scores = extra_credit + jax.random.permutation(key_priority, worker_count)
        chosen = jnp.argsort(-owner_scores)[:CB]
        return chosen[jax.random.permutation(key_mix, CB)]
    return jax.vmap(one_row)(jax.random.split(key_rows, RB)).astype(jnp.int32)


def draw_statistics(key, part):
    key = jax.random.fold_in(key, 5)
    key_diag, key_noise = jax.random.split(key)
    leading = (N_FSDP * N_REP, SLOTS, 2)
    diagonal = jnp.exp(jax.random.uniform(key_diag, leading + (B,), jnp.float32, math.log(5.0), math.log(40.0)))
    noise = jax.random.normal(key_noise, leading + (B, B), jnp.float32)
    return assemble(diagonal, noise)


def draw_inverse_fourth_roots(key, part):
    key = jax.random.fold_in(key, 7)
    key_diag, key_noise = jax.random.split(key)
    leading = (N_FSDP * N_REP, SLOTS, 2)
    diagonal = jnp.exp(jax.random.uniform(key_diag, leading + (B,), jnp.float32, math.log(0.25), math.log(1.0)))
    noise = jax.random.normal(key_noise, leading + (B, B), jnp.float32)
    return assemble(diagonal, noise).astype(jnp.bfloat16)


def shard_levels(own_key, extent, cuts, low, top_value):
    def one(position, blocks):
        draws = jax.random.uniform(jax.random.fold_in(jax.random.fold_in(own_key, 6), position), (blocks,), jnp.float32, low / len(cuts), top_value / len(cuts))
        return jnp.repeat(jnp.exp(draws), extent[position] // blocks).reshape((-1,) + (1,) * (len(extent) - position - 1))

    level = one(*cuts[0])
    for cut in cuts[1:]:
        level = level * one(*cut)
    return level


def centred(rng, extent, deviation, most, cuts=(), kind=jnp.bfloat16):
    drawn = jax.random.normal(rng, extent, jnp.float32) * deviation
    if len(cuts) > 0:
        drawn = shard_levels(rng, extent, cuts, -0.22, 0.18) * drawn
    return jnp.clip(drawn, min=-most, max=most).astype(kind)


def setup_inputs(seed: int = 0) -> dict:
    key_of = jax.random.split(jax.random.key(seed), 5)
    return {
        "gradient": centred(key_of[0], (N_REP, ROWS, COLS), 0.1, 0.6, ((0, 4), (1, 32)), jnp.float32),
        "block_owner_table": draw_block_owner_table(jax.random.fold_in(key_of[4], 71), 0),
        "statistics": draw_statistics(jax.random.fold_in(key_of[4], 71), 0),
        "inverse_fourth_roots": draw_inverse_fourth_roots(jax.random.fold_in(key_of[4], 71), 0),
    }


BETA = 0.9
EPS = 1e-06

def precondition(matrix, statistic, inverse_pair):
    highest = lax.Precision.HIGHEST
    left_gram = jnp.dot(matrix, matrix.T, precision=highest, preferred_element_type=jnp.float32)
    right_gram = jnp.dot(matrix.T, matrix, precision=highest, preferred_element_type=jnp.float32)
    renewed = jnp.stack([BETA * statistic[0] + (1.0 - BETA) * left_gram, BETA * statistic[1] + (1.0 - BETA) * right_gram])
    left_root = inverse_pair[0].astype(jnp.float32)
    right_root = inverse_pair[1].astype(jnp.float32)
    shaped = jnp.dot(jnp.dot(left_root, matrix, precision=highest, preferred_element_type=jnp.float32), right_root, precision=highest, preferred_element_type=jnp.float32)
    factor = jnp.sqrt(jnp.mean(matrix * matrix)) / jnp.sqrt(jnp.mean(shaped * shaped) + EPS)
    return (renewed, shaped * factor)

def reference(gradient, block_owner_table, statistics, inverse_fourth_roots):
    summed = lax.optimization_barrier(jnp.sum(gradient, axis=0))
    row_count = summed.shape[0]
    col_count = summed.shape[1]
    row_blocks = row_count // B
    col_blocks = col_count // B
    worker_count = N_FSDP * N_REP
    blocks = summed.reshape(row_blocks, B, col_blocks, B).transpose(0, 2, 1, 3).reshape(row_blocks * col_blocks, B, B)
    holding = jnp.any(block_owner_table[:, :, None] == jnp.arange(worker_count, dtype=jnp.int32)[None, None, :], axis=1).astype(jnp.int32)
    before = jnp.cumsum(holding, axis=0) - holding
    slot_rank = jnp.take_along_axis(before, block_owner_table, axis=1).astype(jnp.int32)
    flat_owner = block_owner_table.reshape(-1).astype(jnp.int32)
    flat_slot = slot_rank.reshape(-1)

    def one_block(record):
        matrix, where_dev, where_slot = record
        return precondition(matrix, statistics[where_dev, where_slot], inverse_fourth_roots[where_dev, where_slot])
    renewed, updated = lax.map(one_block, (blocks, flat_owner, flat_slot))
    new_statistics = jnp.zeros(statistics.shape, jnp.float32).at[flat_owner, flat_slot].set(renewed)
    direction = updated.reshape(row_blocks, col_blocks, B, B).transpose(0, 2, 1, 3).reshape(row_count, col_count)
    return (direction, new_statistics)
```

```python
import functools

import jax
import jax.numpy as jnp
from jax import lax
from jax.experimental import pallas as pl
from jax.experimental.pallas import tpu as pltpu
from jax.sharding import PartitionSpec as P

BETA = 0.9
EPS = 1e-06


def split(value):
    high = value.astype(jnp.bfloat16)
    low = (value - high.astype(jnp.float32)).astype(jnp.bfloat16)
    return high, low


def dot(a, b):
    return jnp.dot(a, b, preferred_element_type=jnp.float32)


def dot_t(a, b):
    return lax.dot_general(a, b, (((1,), (1,)), ((), ())), preferred_element_type=jnp.float32)


def block_kernel(row_ref, live_ref, g_ref, stat_ref, root_ref, new_ref, out_ref):
    live = live_ref[pl.program_id(0)] > 0

    @pl.when(live)
    def _():
        matrix = g_ref[0]
        size = matrix.shape[0]
        high, low = split(matrix)
        half = high * jnp.bfloat16(0.5)
        left = dot_t(high, half) + dot_t(high, low)
        new_ref[0, 0, 0] = BETA * stat_ref[0, 0, 0] + (1.0 - BETA) * (left + left.T)
        high_t = high.T
        right = dot(high_t, half) + dot(high_t, low)
        new_ref[0, 0, 1] = BETA * stat_ref[0, 0, 1] + (1.0 - BETA) * (right + right.T)
        left_root = root_ref[0, 0, 0]
        right_root = root_ref[0, 0, 1]
        t_high, t_low = split(dot(left_root, high) + dot(left_root, low))
        shaped = dot(t_high, right_root) + dot(t_low, right_root)
        count = size * size
        square_g = jnp.sum(matrix * matrix, keepdims=True) / count
        square_s = jnp.sum(shaped * shaped, keepdims=True) / count
        out_ref[0] = shaped * (jnp.sqrt(square_g) / jnp.sqrt(square_s + EPS))

    @pl.when(jnp.logical_not(live))
    def _():
        new_ref[...] = jnp.zeros_like(new_ref)
        out_ref[...] = jnp.zeros_like(out_ref)


def precondition(row_of_slot, live, blocks, statistics, roots):
    slots, size = statistics.shape[1], statistics.shape[3]
    square = (1, size, size)
    pair = (1, 1, 2, size, size)
    by_row = pl.BlockSpec(square, lambda s, row, live: (row[s], 0, 0))
    by_slot = pl.BlockSpec(pair, lambda s, row, live: (0, s, 0, 0, 0))
    return pl.pallas_call(
        block_kernel,
        grid_spec=pltpu.PrefetchScalarGridSpec(
            num_scalar_prefetch=2,
            grid=(slots,),
            in_specs=[by_row, by_slot, by_slot],
            out_specs=[by_slot, by_row],
        ),
        out_shape=(
            jax.ShapeDtypeStruct(statistics.shape, jnp.float32),
            jax.ShapeDtypeStruct(blocks.shape, jnp.float32),
        ),
        compiler_params=pltpu.CompilerParams(vmem_limit_bytes=48 * 2**20),
        name="precondition",
    )(row_of_slot, live, blocks, statistics, roots)


def slot_order(mine):
    owned = jnp.any(mine, axis=1)
    count = owned.astype(jnp.int32)
    free = 1 - count
    slot_of_row = jnp.where(
        owned, jnp.cumsum(count) - count, jnp.sum(count) + jnp.cumsum(free) - free
    )
    rows = jnp.arange(count.shape[0], dtype=jnp.int32)
    match = slot_of_row[None, :] == rows[:, None]
    row_of_slot = jnp.sum(jnp.where(match, rows[None, :], 0), axis=1)
    live = (rows < jnp.sum(count)).astype(jnp.int32)
    return row_of_slot, live


def on_device(gradient, block_owner_table, statistics, inverse_fourth_roots):
    fsdp_size = lax.axis_size("fsdp")
    rep_size = lax.axis_size("rep")
    workers = fsdp_size * rep_size
    fsdp_index = lax.axis_index("fsdp")
    rep_index = lax.axis_index("rep")
    size = statistics.shape[3]
    row_blocks, col_blocks = block_owner_table.shape
    shard_rows = gradient.shape[1]
    piece_rows = shard_rows // rep_size
    table = block_owner_table

    row_owners = lax.dynamic_index_in_dim(
        table, fsdp_index * shard_rows // size, 0, keepdims=False
    )
    row_of_slot, live = slot_order(table == fsdp_index * rep_size + rep_index)
    matches = row_owners[None, :] == jnp.arange(workers, dtype=jnp.int32)[:, None]
    columns = jnp.arange(col_blocks, dtype=jnp.int32)
    picked = jnp.sum(jnp.where(matches, columns[None, :], 0), axis=1)

    summed = lax.psum_scatter(gradient[0], "rep", scatter_dimension=0, tiled=True)
    pieces = summed.reshape(piece_rows, col_blocks, size).transpose(1, 0, 2)
    outgoing = jnp.take(pieces, picked, axis=0)
    arrived = lax.all_to_all(outgoing, ("fsdp", "rep"), split_axis=0, concat_axis=0, tiled=True)
    blocks = arrived.reshape(row_blocks, size, size)
    new_statistics, updated = precondition(
        row_of_slot, live, blocks, statistics, inverse_fourth_roots
    )
    returning = updated.reshape(workers, piece_rows, size)
    came_back = lax.all_to_all(returning, ("fsdp", "rep"), split_axis=0, concat_axis=0, tiled=True)
    ordered = jnp.take(came_back, row_owners, axis=0)
    quarter = lax.all_to_all(ordered, "rep", split_axis=0, concat_axis=1, tiled=True)
    direction = quarter.transpose(1, 0, 2).reshape(shard_rows, -1)
    return (direction, new_statistics)


def solution(mesh):
    in_specs = (
        P("rep", "fsdp", None),
        P(),
        P(("fsdp", "rep"), None, None, None, None),
        P(("fsdp", "rep"), None, None, None, None),
    )
    out_specs = (P("fsdp", "rep"), P(("fsdp", "rep"), None, None, None, None))
    return jax.shard_map(
        on_device, mesh=mesh, in_specs=in_specs, out_specs=out_specs, check_vma=False
    )
```

```python
import functools
import itertools

import jax
import jax.numpy as jnp
from jax import lax
from jax.experimental import pallas as pl
from jax.experimental.pallas import tpu as pltpu
from jax.sharding import PartitionSpec as P

BETA = 0.9
EPS = 1e-06
MESH = pl.DeviceIdType.MESH
RING = 4
CORES = 2
PARTS = 4


def far_first():
    seen, orbits = set(), []
    for start in itertools.product(range(RING), repeat=3):
        if start in seen:
            continue
        orbit, turned = [], start
        for _ in range(3):
            for offset in (turned, tuple(-v % RING for v in turned)):
                if offset not in orbit:
                    orbit.append(offset)
            turned = turned[1:] + turned[:1]
        seen.update(orbit)
        orbits.append(orbit)
    orbits.sort(key=lambda orbit: -sum(min(v, RING - v) for v in orbit[0]))
    order = [(z, x, c, y) for orbit in orbits for c in range(CORES) for z, x, y in orbit]
    return [offset for offset in order if any(offset)]


ORDER = far_first()


class Place:
    def __init__(self):
        fsdp, self.y = lax.axis_index("fsdp"), lax.axis_index("rep")
        self.z, self.x, self.c = fsdp // 8, fsdp // 2 % 4, fsdp % 2
        self.shard = fsdp % 8
        self.index = fsdp * RING + self.y
        self.zs = [lax.rem(self.z + d, RING) for d in range(RING)]
        self.xs = [lax.rem(self.x + d, RING) * CORES for d in range(RING)]
        self.cs = [self.c, 1 - self.c]
        self.ys = [lax.rem(self.y + d, RING) for d in range(RING)]

    def at(self, dz, dx, dc, dy):
        shard = self.xs[dx] + self.cs[dc]
        z, y = self.zs[dz], self.ys[dy]
        return z, shard * RING + y, (z * 8 + shard, y)

    def line(self, dy):
        return {"rep": self.ys[dy]}


def greet_all(place):
    barrier = pltpu.get_barrier_semaphore()
    for offset in ORDER:
        pl.semaphore_signal(barrier, inc=1, device_id=place.at(*offset)[2], device_id_type=MESH)
    pl.semaphore_wait(barrier, len(ORDER))


def send(src, dst, sent, landed, device):
    copy = pltpu.make_async_remote_copy(
        src_ref=src,
        dst_ref=dst,
        send_sem=sent,
        recv_sem=landed,
        device_id=device,
        device_id_type=MESH,
    )
    copy.start()


def await_bytes(like, semaphore):
    pltpu.make_async_copy(like, like, semaphore).wait()


def dispatch_kernel(
    picked_ref, grad_ref, out_ref,
    near, mine, relay, coming, pieces, stage,
    load_sem, sent_sem, relay_sent_sem, relay_sem, coming_sem, out_sent_sem, out_sem,
):
    place = Place()
    rows, half = mine.shape[0], mine.shape[1] // 2
    width = half // PARTS
    size = stage.shape[2]

    def quarter(dy):
        return pl.ds(pl.multiple_of(place.ys[dy] * rows, rows), rows)

    def grad(dy, side, part=None):
        start, count = (side * half, half) if part is None else (side * half + part * width, width)
        return grad_ref.at[0, quarter(dy), pl.ds(start, count)]

    loads = [
        pltpu.make_async_copy(grad(1, 0), near.at[0], load_sem.at[0]),
        pltpu.make_async_copy(grad(3, 1), near.at[1], load_sem.at[1]),
        pltpu.make_async_copy(grad_ref.at[0, quarter(0)], mine, load_sem.at[2]),
    ]
    for load in loads:
        load.start()
    greet_all(place)

    ways = ((1, 0), (3, 1))
    for part in range(PARTS):
        for to, side in ways:
            send(
                grad(2, side, part), relay.at[side, :, pl.ds(part * width, width)],
                sent_sem, relay_sem.at[side, part], place.line(to),
            )
    for part in range(PARTS):
        for to, side in ways:
            columns = pl.ds((1 - side) * half + part * width, width)
            send(
                grad(to, 1 - side, part), coming.at[side, :, columns],
                sent_sem, coming_sem.at[side, 1 - side, part], place.line(to),
            )
    for load in loads:
        load.wait()
    for part in range(PARTS):
        for to, side in ways:
            here = pl.ds(part * width, width)
            block = relay.at[side, :, here]
            await_bytes(block, relay_sem.at[side, part])
            relay[side, :, here] += near[side, :, here]
            columns = pl.ds(side * half + part * width, width)
            send(
                block, coming.at[side, :, columns],
                relay_sent_sem, coming_sem.at[side, side, part], place.line(to),
            )
    for side in range(2):
        for part in range(PARTS):
            columns = pl.ds((1 - side) * half + part * width, width)
            await_bytes(coming.at[side, :, columns], coming_sem.at[side, 1 - side, part])
            mine[:, columns] += coming[side, :, columns]
    for part in range(PARTS):
        for side in range(2):
            start = side * half + part * width
            columns = pl.ds(start, width)
            await_bytes(coming.at[side, :, columns], coming_sem.at[side, side, part])
            for column in range(start, start + width, size):
                at = pl.ds(column, size)
                pieces[column // size] = mine[:, at] + coming[side, :, at]

    chunk = pl.ds(pl.multiple_of((place.shard * RING + place.y) * rows, rows), rows)
    landing = out_ref.at[place.z, chunk]
    for offset in ORDER:
        z, k, device = place.at(*offset)
        target = z * 32 + k
        stage[target] = pieces[picked_ref[target]]
        send(stage.at[target], landing, out_sent_sem, out_sem.at[place.z], device)
    stage[place.index] = pieces[picked_ref[place.index]]
    pltpu.make_async_copy(stage.at[place.index], landing, out_sem.at[place.z]).start()
    for row_block in range(RING):
        await_bytes(out_ref.at[row_block], out_sem.at[row_block])
    await_bytes(mine, relay_sent_sem)
    await_bytes(coming, sent_sem)
    await_bytes(stage.at[pl.ds(0, len(ORDER))], out_sent_sem)


def dispatch(picked, gradient, size):
    _, shard_rows, columns = gradient.shape
    rows = shard_rows // RING
    return pl.pallas_call(
        dispatch_kernel,
        out_shape=jax.ShapeDtypeStruct((RING, size, size), jnp.float32),
        in_specs=[
            pl.BlockSpec(memory_space=pltpu.SMEM),
            pl.BlockSpec(memory_space=pl.ANY),
        ],
        out_specs=pl.BlockSpec(memory_space=pl.ANY),
        scratch_shapes=[
            pltpu.VMEM((2, rows, columns // 2), jnp.float32),
            pltpu.VMEM((rows, columns), jnp.float32),
            pltpu.VMEM((2, rows, columns // 2), jnp.float32),
            pltpu.VMEM((2, rows, columns), jnp.float32),
            pltpu.VMEM((columns // size, rows, size), jnp.float32),
            pltpu.VMEM((len(ORDER) + 1, rows, size), jnp.float32),
            pltpu.SemaphoreType.DMA((3,)),
            pltpu.SemaphoreType.DMA,
            pltpu.SemaphoreType.DMA,
            pltpu.SemaphoreType.DMA((2, PARTS)),
            pltpu.SemaphoreType.DMA((2, 2, PARTS)),
            pltpu.SemaphoreType.DMA,
            pltpu.SemaphoreType.DMA((RING,)),
        ],
        compiler_params=pltpu.CompilerParams(
            collective_id=0, has_side_effects=True, vmem_limit_bytes=32 * 2**20
        ),
        name="dispatch",
    )(picked, gradient)


def return_kernel(
    owners_ref, updated_ref, out_ref,
    came, final, came_sent_sem, came_sem, final_sent_sem, out_sem,
):
    place = Place()
    rows, size = came.shape[1:]
    greet_all(place)

    def piece(z, k):
        return updated_ref.at[z, pl.ds(pl.multiple_of(k * rows, rows), rows)]

    landing = came.at[place.index]
    own = pltpu.make_async_copy(
        piece(place.z, place.shard * RING + place.y), landing, came_sem
    )
    own.start()
    for offset in ORDER:
        z, k, device = place.at(*offset)
        send(piece(z, k), landing, came_sent_sem, came_sem, device)
    await_bytes(came, came_sem)

    per_quarter = final.shape[2] // size
    out_rows = out_ref.at[pl.ds(pl.multiple_of(place.y * rows, rows), rows)]
    for dy in (2, 1, 3, 0):
        for column in range(per_quarter):
            owner = owners_ref[place.ys[dy] * per_quarter + column]
            final[dy, :, pl.ds(column * size, size)] = came[owner]
        if dy:
            send(final.at[dy], out_rows, final_sent_sem, out_sem, place.line(dy))
        else:
            pltpu.make_async_copy(final.at[dy], out_rows, out_sem).start()
    await_bytes(out_ref, out_sem)
    await_bytes(came.at[pl.ds(0, len(ORDER))], came_sent_sem)
    await_bytes(final.at[pl.ds(0, RING - 1)], final_sent_sem)


def give_back(owners, updated, shard_rows, columns):
    size = updated.shape[2]
    rows = shard_rows // RING
    return pl.pallas_call(
        return_kernel,
        out_shape=jax.ShapeDtypeStruct((shard_rows, columns), jnp.float32),
        in_specs=[
            pl.BlockSpec(memory_space=pltpu.SMEM),
            pl.BlockSpec(memory_space=pl.ANY),
        ],
        out_specs=pl.BlockSpec(memory_space=pl.ANY),
        scratch_shapes=[
            pltpu.VMEM((len(ORDER) + 1, rows, size), jnp.float32),
            pltpu.VMEM((RING, rows, columns), jnp.float32),
            pltpu.SemaphoreType.DMA,
            pltpu.SemaphoreType.DMA,
            pltpu.SemaphoreType.DMA,
            pltpu.SemaphoreType.DMA,
        ],
        compiler_params=pltpu.CompilerParams(
            collective_id=1, has_side_effects=True, vmem_limit_bytes=32 * 2**20
        ),
        name="give_back",
    )(owners, updated)


def split(value):
    high = value.astype(jnp.bfloat16)
    low = (value - high.astype(jnp.float32)).astype(jnp.bfloat16)
    return high, low


def dot(a, b):
    return jnp.dot(a, b, preferred_element_type=jnp.float32)


def dot_t(a, b):
    return lax.dot_general(a, b, (((1,), (1,)), ((), ())), preferred_element_type=jnp.float32)


def block_kernel(row_ref, live_ref, g_ref, stat_ref, root_ref, new_ref, out_ref):
    live = live_ref[pl.program_id(0)] > 0

    @pl.when(live)
    def _():
        matrix = g_ref[0]
        size = matrix.shape[0]
        high, low = split(matrix)
        half = high * jnp.bfloat16(0.5)
        left = dot_t(high, half) + dot_t(high, low)
        new_ref[0, 0, 0] = BETA * stat_ref[0, 0, 0] + (1.0 - BETA) * (left + left.T)
        high_t = high.T
        right = dot(high_t, half) + dot(high_t, low)
        new_ref[0, 0, 1] = BETA * stat_ref[0, 0, 1] + (1.0 - BETA) * (right + right.T)
        left_root = root_ref[0, 0, 0]
        right_root = root_ref[0, 0, 1]
        t_high, t_low = split(dot(left_root, high) + dot(left_root, low))
        shaped = dot(t_high, right_root) + dot(t_low, right_root)
        count = size * size
        square_g = jnp.sum(matrix * matrix, keepdims=True) / count
        square_s = jnp.sum(shaped * shaped, keepdims=True) / count
        out_ref[0] = shaped * (jnp.sqrt(square_g) / jnp.sqrt(square_s + EPS))

    @pl.when(jnp.logical_not(live))
    def _():
        new_ref[...] = jnp.zeros_like(new_ref)
        out_ref[...] = jnp.zeros_like(out_ref)


def precondition(row_of_slot, live, blocks, statistics, roots):
    slots, size = statistics.shape[1], statistics.shape[3]
    square = (1, size, size)
    pair = (1, 1, 2, size, size)
    by_row = pl.BlockSpec(square, lambda s, row, live: (row[s], 0, 0))
    by_slot = pl.BlockSpec(pair, lambda s, row, live: (0, s, 0, 0, 0))
    return pl.pallas_call(
        block_kernel,
        grid_spec=pltpu.PrefetchScalarGridSpec(
            num_scalar_prefetch=2,
            grid=(slots,),
            in_specs=[by_row, by_slot, by_slot],
            out_specs=[by_slot, by_row],
        ),
        out_shape=(
            jax.ShapeDtypeStruct(statistics.shape, jnp.float32),
            jax.ShapeDtypeStruct(blocks.shape, jnp.float32),
        ),
        compiler_params=pltpu.CompilerParams(vmem_limit_bytes=48 * 2**20),
        name="precondition",
    )(row_of_slot, live, blocks, statistics, roots)


def slot_order(mine):
    owned = jnp.any(mine, axis=1)
    count = owned.astype(jnp.int32)
    free = 1 - count
    slot_of_row = jnp.where(
        owned, jnp.cumsum(count) - count, jnp.sum(count) + jnp.cumsum(free) - free
    )
    rows = jnp.arange(count.shape[0], dtype=jnp.int32)
    match = slot_of_row[None, :] == rows[:, None]
    row_of_slot = jnp.sum(jnp.where(match, rows[None, :], 0), axis=1)
    live = (rows < jnp.sum(count)).astype(jnp.int32)
    return row_of_slot, live


def on_device(gradient, block_owner_table, statistics, inverse_fourth_roots):
    fsdp_size = lax.axis_size("fsdp")
    rep_size = lax.axis_size("rep")
    workers = fsdp_size * rep_size
    fsdp_index = lax.axis_index("fsdp")
    rep_index = lax.axis_index("rep")
    size = statistics.shape[3]
    col_blocks = block_owner_table.shape[1]
    shard_rows, columns = gradient.shape[1:]
    table = block_owner_table

    row_owners = lax.dynamic_index_in_dim(
        table, fsdp_index * shard_rows // size, 0, keepdims=False
    )
    row_of_slot, live = slot_order(table == fsdp_index * rep_size + rep_index)
    matches = row_owners[None, :] == jnp.arange(workers, dtype=jnp.int32)[:, None]
    column_index = jnp.arange(col_blocks, dtype=jnp.int32)
    picked = jnp.sum(jnp.where(matches, column_index[None, :], 0), axis=1)

    blocks = dispatch(picked, gradient, size)
    new_statistics, updated = precondition(
        row_of_slot, live, blocks, statistics, inverse_fourth_roots
    )
    direction = give_back(row_owners, updated, shard_rows, columns // rep_size)
    return (direction, new_statistics)


def solution(mesh):
    in_specs = (
        P("rep", "fsdp", None),
        P(),
        P(("fsdp", "rep"), None, None, None, None),
        P(("fsdp", "rep"), None, None, None, None),
    )
    out_specs = (P("fsdp", "rep"), P(("fsdp", "rep"), None, None, None, None))
    return jax.shard_map(
        on_device, mesh=mesh, in_specs=in_specs, out_specs=out_specs, check_vma=False
    )
```

```python
import itertools

import jax
import jax.numpy as jnp
from jax import lax
from jax.experimental import pallas as pl
from jax.experimental.pallas import tpu as pltpu
from jax.sharding import PartitionSpec as P

BETA = 0.9
EPS = 1e-06
MESH = pl.DeviceIdType.MESH
RING = 4
CORES = 2
SHARDS = RING * CORES
PLANE = SHARDS * RING
PARTS = 4


def balanced(offsets):
    left, order, load = sorted(offsets), [], [0.0] * 6

    def hops(offset):
        dz, dx, _, dy = offset
        steps = []
        for d in (dz, dx, dy):
            steps += [1, 1] if d == 2 else [d == 1, d == 3]
        return steps

    while left:
        def cost(offset):
            after = [a + b for a, b in zip(load, hops(offset))]
            return (max(after) - sum(after) / 6, -sum(hops(offset)), offset)

        best = min(left, key=cost)
        left.remove(best)
        order.append(best)
        load = [a + b for a, b in zip(load, hops(best))]
    return order


def offsets(planes):
    every = itertools.product(planes, range(RING), range(CORES), range(RING))
    return [offset for offset in every if any(offset)]


SECOND = balanced(offsets((1, 3)))
ORDER = balanced(offsets((0, 2))) + SECOND


class Place:
    def __init__(self):
        fsdp, self.y = lax.axis_index("fsdp"), lax.axis_index("rep")
        self.z = fsdp // SHARDS
        self.shard = fsdp % SHARDS
        self.chunk = self.shard * RING + self.y
        self.index = fsdp * RING + self.y
        x, c = self.shard // CORES, self.shard % CORES
        self.zs = [lax.rem(self.z + d, RING) for d in range(RING)]
        self.xs = [lax.rem(x + d, RING) * CORES for d in range(RING)]
        self.cs = [c, 1 - c]
        self.ys = [lax.rem(self.y + d, RING) for d in range(RING)]

    def in_plane(self, dx, dc, dy):
        shard = self.xs[dx] + self.cs[dc]
        return shard, self.ys[dy]

    def line(self, dy):
        return {"rep": self.ys[dy]}


def send(src, dst, sent, landed, device):
    pltpu.make_async_remote_copy(
        src_ref=src,
        dst_ref=dst,
        send_sem=sent,
        recv_sem=landed,
        device_id=device,
        device_id_type=MESH,
    ).start()


def await_bytes(like, semaphore):
    pltpu.make_async_copy(like, like, semaphore).wait()


def split(value):
    high = value.astype(jnp.bfloat16)
    low = (value - high.astype(jnp.float32)).astype(jnp.bfloat16)
    return high, low


def dot(a, b):
    return jnp.dot(a, b, preferred_element_type=jnp.float32)


def dot_t(a, b):
    return lax.dot_general(a, b, (((1,), (1,)), ((), ())), preferred_element_type=jnp.float32)


def grafted(matrix, left_root, right_root):
    high, low = split(matrix)
    t_high, t_low = split(dot(left_root, high) + dot(left_root, low))
    shaped = dot(t_high, right_root) + dot(t_low, right_root)
    square_g = jnp.sum(matrix * matrix, keepdims=True) / matrix.size
    square_s = jnp.sum(shaped * shaped, keepdims=True) / matrix.size
    return shaped * (jnp.sqrt(square_g) / jnp.sqrt(square_s + EPS))


def half_grams(matrix):
    high, low = split(matrix)
    half = high * jnp.bfloat16(0.5)
    left = dot_t(high, half) + dot_t(high, low)
    high_t = high.T
    right = dot(high_t, half) + dot(high_t, low)
    return left, right


def pick(index, values):
    result = values[0]
    for k in range(1, len(values)):
        result = jnp.where(index == k, values[k], result)
    return result


def step_kernel(
    table_ref, grad_ref, stat_ref, root_ref, direction_ref, new_ref,
    near, mine, relay, coming, pieces, stage, blocks, roots, returning, came, final,
    picked_row, picked,
    load_sem, sent_sem, relay_sent_sem, relay_sem, coming_sem, out_sent_sem, out_sem,
    back_sent_sem, back_sem, final_sent_sem, final_sem,
):
    place = Place()
    rows, half = mine.shape[0], mine.shape[1] // 2
    width = half // PARTS
    size = stage.shape[2]
    row_blocks, col_blocks = table_ref.shape

    def quarter(dy):
        return pl.ds(pl.multiple_of(place.ys[dy] * rows, rows), rows)

    def grad(dy, side, part=None):
        start, count = (side * half, half) if part is None else (side * half + part * width, width)
        return grad_ref.at[0, quarter(dy), pl.ds(start, count)]

    loads = [
        pltpu.make_async_copy(grad(1, 0), near.at[0], load_sem.at[0]),
        pltpu.make_async_copy(grad(3, 1), near.at[1], load_sem.at[1]),
        pltpu.make_async_copy(grad_ref.at[0, quarter(0)], mine, load_sem.at[2]),
    ]
    root_load = pltpu.make_async_copy(root_ref.at[0], roots, load_sem.at[3])
    stat_load = pltpu.make_async_copy(stat_ref, new_ref, load_sem.at[4])
    for load in loads:
        load.start()

    barrier = pltpu.get_barrier_semaphore()
    for dz, dx, dc, dy in ORDER:
        shard, y = place.in_plane(dx, dc, dy)
        device = (place.zs[dz] * SHARDS + shard, y)
        pl.semaphore_signal(barrier, inc=1, device_id=device, device_id_type=MESH)
    pl.semaphore_wait(barrier, len(ORDER))

    ways = ((1, 0), (3, 1))
    for part in range(PARTS):
        for to, side in ways:
            send(
                grad(2, side, part), relay.at[side, :, pl.ds(part * width, width)],
                sent_sem, relay_sem.at[side, part], place.line(to),
            )
    for part in range(PARTS):
        for to, side in ways:
            columns = pl.ds((1 - side) * half + part * width, width)
            send(
                grad(to, 1 - side, part), coming.at[side, :, columns],
                sent_sem, coming_sem.at[side, 1 - side, part], place.line(to),
            )

    lanes = lax.broadcasted_iota(jnp.int32, picked_row.shape, 1)
    columns_of = jnp.zeros(picked_row.shape, jnp.int32)
    for column in range(col_blocks):
        columns_of = jnp.where(lanes == table_ref[place.z, column], column, columns_of)
    picked_row[...] = columns_of
    picked_copy = pltpu.make_async_copy(picked_row, picked, load_sem.at[5])
    picked_copy.start()

    owned, slot_of_row = [], []
    total = jnp.int32(0)
    for row in range(row_blocks):
        count = jnp.int32(0)
        for column in range(col_blocks):
            count = jnp.where(table_ref[row, column] == place.index, 1, count)
        owned.append(count)
        slot_of_row.append(total)
        total += count
    row_of_slot = []
    for slot in range(row_blocks):
        row_of = jnp.int32(0)
        for row in range(row_blocks):
            row_of += jnp.where(slot_of_row[row] == slot, owned[row] * row, 0)
        row_of_slot.append(row_of)

    for load in loads:
        load.wait()
    for part in range(PARTS):
        for to, side in ways:
            here = pl.ds(part * width, width)
            block = relay.at[side, :, here]
            await_bytes(block, relay_sem.at[side, part])
            relay[side, :, here] += near[side, :, here]
            columns = pl.ds(side * half + part * width, width)
            send(
                block, coming.at[side, :, columns],
                relay_sent_sem, coming_sem.at[side, side, part], place.line(to),
            )
    root_load.start()
    stat_load.start()
    picked_copy.wait()
    for side in range(2):
        for part in range(PARTS):
            columns = pl.ds((1 - side) * half + part * width, width)
            await_bytes(coming.at[side, :, columns], coming_sem.at[side, 1 - side, part])
            mine[:, columns] += coming[side, :, columns]
    for part in range(PARTS):
        for side in range(2):
            start = side * half + part * width
            columns = pl.ds(start, width)
            await_bytes(coming.at[side, :, columns], coming_sem.at[side, side, part])
            for column in range(start, start + width, size):
                at = pl.ds(column, size)
                pieces[column // size] = mine[:, at] + coming[side, :, at]

    chunk = pl.ds(pl.multiple_of(place.chunk * rows, rows), rows)
    landing = blocks.at[place.z, chunk]
    for dz, dx, dc, dy in ORDER:
        shard, y = place.in_plane(dx, dc, dy)
        fsdp = place.zs[dz] * SHARDS + shard
        target = fsdp * RING + y
        stage[target] = pieces[picked[0, target]]
        send(stage.at[target], landing, out_sent_sem, out_sem.at[place.z], (fsdp, y))
    stage[place.index] = pieces[picked[0, place.index]]
    pltpu.make_async_copy(stage.at[place.index], landing, out_sem.at[place.z]).start()

    root_load.wait()
    landing_back = came.at[place.index]

    def two_rows(step, carry):
        planes = [jnp.where(step == 0, 2, 1), jnp.where(step == 0, 0, 3)]
        block_rows = [lax.rem(place.z + dz, RING) for dz in planes]
        for row in block_rows:
            await_bytes(blocks.at[row], out_sem.at[row])
            slot = pick(row, slot_of_row)
            returning[row] = grafted(blocks[row], roots[slot, 0], roots[slot, 1])
        for dz, dx, dc, dy in SECOND:
            row = block_rows[dz // 2]
            shard, y = place.in_plane(dx, dc, dy)
            start = pl.multiple_of((shard * RING + y) * rows, rows)
            piece = returning.at[row, pl.ds(start, rows)]

            def away(piece=piece, row=row, shard=shard, y=y):
                send(piece, landing_back, back_sent_sem, back_sem, (row * SHARDS + shard, y))

            if dz == 1 or any((dx, dc, dy)):
                away()
            else:
                pl.when(step != 0)(away)

                @pl.when(step == 0)
                def _():
                    pltpu.make_async_copy(piece, landing_back, back_sem).start()
        return carry

    lax.fori_loop(0, row_blocks // 2, two_rows, 0)

    stat_load.wait()

    def one_slot(slot, carry):
        left, right = half_grams(blocks[pick(slot, row_of_slot)])
        live = slot < total
        for k, gram in enumerate((left, right)):
            renewed = BETA * new_ref[0, slot, k] + (1.0 - BETA) * (gram + gram.T)
            new_ref[0, slot, k] = jnp.where(live, renewed, 0.0)
        return carry

    lax.fori_loop(0, row_blocks, one_slot, 0)

    await_bytes(came, back_sem)
    per_quarter = final.shape[2] // size
    out_rows = direction_ref.at[pl.ds(pl.multiple_of(place.y * rows, rows), rows)]
    for dy in (2, 1, 3, 0):
        for column in range(per_quarter):
            owner = table_ref[place.z, place.ys[dy] * per_quarter + column]
            final[dy, :, pl.ds(column * size, size)] = came[owner]
        if dy:
            send(final.at[dy], out_rows, final_sent_sem, final_sem, place.line(dy))
        else:
            pltpu.make_async_copy(final.at[dy], out_rows, final_sem).start()

    await_bytes(mine, relay_sent_sem)
    await_bytes(coming, sent_sem)
    await_bytes(stage.at[pl.ds(0, len(ORDER))], out_sent_sem)
    await_bytes(came.at[pl.ds(0, len(ORDER))], back_sent_sem)
    await_bytes(final.at[pl.ds(0, RING - 1)], final_sent_sem)
    await_bytes(direction_ref, final_sem)


def on_device(gradient, block_owner_table, statistics, inverse_fourth_roots):
    size = statistics.shape[3]
    row_blocks, col_blocks = block_owner_table.shape
    _, shard_rows, columns = gradient.shape
    rows = shard_rows // RING
    workers = RING * PLANE
    dma = pltpu.SemaphoreType.DMA
    anywhere = pl.BlockSpec(memory_space=pl.ANY)
    return pl.pallas_call(
        step_kernel,
        out_shape=(
            pltpu.VMEM((shard_rows, columns // RING), jnp.float32),
            pltpu.VMEM(statistics.shape, jnp.float32),
        ),
        in_specs=[pl.BlockSpec(memory_space=pltpu.SMEM), anywhere, anywhere, anywhere],
        out_specs=(pl.BlockSpec(memory_space=pltpu.VMEM),) * 2,
        scratch_shapes=[
            pltpu.VMEM((2, rows, columns // 2), jnp.float32),
            pltpu.VMEM((rows, columns), jnp.float32),
            pltpu.VMEM((2, rows, columns // 2), jnp.float32),
            pltpu.VMEM((2, rows, columns), jnp.float32),
            pltpu.VMEM((col_blocks, rows, size), jnp.float32),
            pltpu.VMEM((workers, rows, size), jnp.float32),
            pltpu.VMEM((row_blocks, size, size), jnp.float32),
            pltpu.VMEM(inverse_fourth_roots.shape[1:], jnp.bfloat16),
            pltpu.VMEM((row_blocks, size, size), jnp.float32),
            pltpu.VMEM((workers, rows, size), jnp.float32),
            pltpu.VMEM((RING, rows, columns // RING), jnp.float32),
            pltpu.VMEM((1, workers), jnp.int32),
            pltpu.SMEM((1, workers), jnp.int32),
            dma((6,)),
            dma,
            dma,
            dma((2, PARTS)),
            dma((2, 2, PARTS)),
            dma,
            dma((row_blocks,)),
            dma,
            dma,
            dma,
            dma,
        ],
        compiler_params=pltpu.CompilerParams(
            collective_id=0, has_side_effects=True, vmem_limit_bytes=44 * 2**20
        ),
        name="shampoo_step",
    )(block_owner_table, gradient, statistics, inverse_fourth_roots)


def solution(mesh):
    in_specs = (
        P("rep", "fsdp", None),
        P(),
        P(("fsdp", "rep"), None, None, None, None),
        P(("fsdp", "rep"), None, None, None, None),
    )
    out_specs = (P("fsdp", "rep"), P(("fsdp", "rep"), None, None, None, None))
    return jax.shard_map(
        on_device, mesh=mesh, in_specs=in_specs, out_specs=out_specs, check_vma=False
    )
```

```python
import functools
import itertools

import jax
import jax.numpy as jnp
from jax import lax
from jax.experimental import pallas as pl
from jax.experimental.pallas import tpu as pltpu
from jax.sharding import PartitionSpec as P

BETA = 0.9
EPS = 1e-06
MESH = pl.DeviceIdType.MESH
RING = 4
CORES = 2
SHARDS = RING * CORES
PLANE = SHARDS * RING
PARTS = 8
BACK = (8, 8, 8, 8, 8, 8, 8, 8)
EARLY = 3
AHEAD = 3


def balanced(offsets):
    left, order, load = sorted(offsets), [], [0.0] * 6

    def hops(offset):
        dz, dx, _, dy = offset
        steps = []
        for d in (dz, dx, dy):
            steps += [1, 1] if d == 2 else [d == 1, d == 3]
        return steps

    while left:
        def cost(offset):
            after = [a + b for a, b in zip(load, hops(offset))]
            return (max(after) - sum(after) / 6, -sum(hops(offset)), offset)

        best = min(left, key=cost)
        left.remove(best)
        order.append(best)
        load = [a + b for a, b in zip(load, hops(best))]
    return order


def offsets(planes):
    every = itertools.product(planes, range(RING), range(CORES), range(RING))
    return [offset for offset in every if any(offset)]


ORDER = balanced(offsets((0, 2))) + balanced(offsets((1, 3)))
SAME_Y = balanced([offset for offset in offsets(range(RING)) if offset[3] == 0]) + [(0, 0, 0, 0)]
SAME_Y_ODD = [offset for offset in balanced(offsets((1, 3))) if offset[3] == 0]
STARTS = [sum(BACK[:k]) for k in range(len(BACK))]


class Place:
    def __init__(self):
        fsdp, self.y = lax.axis_index("fsdp"), lax.axis_index("rep")
        self.fsdp = fsdp
        self.z = fsdp // SHARDS
        self.shard = fsdp % SHARDS
        self.chunk = self.shard * RING + self.y
        self.index = fsdp * RING + self.y
        x, c = self.shard // CORES, self.shard % CORES
        self.zs = [lax.rem(self.z + d, RING) for d in range(RING)]
        self.xs = [lax.rem(x + d, RING) * CORES for d in range(RING)]
        self.cs = [c, 1 - c]
        self.ys = [lax.rem(self.y + d, RING) for d in range(RING)]

    def in_plane(self, dx, dc, dy):
        shard = self.xs[dx] + self.cs[dc]
        return shard, self.ys[dy]

    def line(self, dy):
        return {"rep": self.ys[dy]}


def send(src, dst, sent, landed, device):
    pltpu.make_async_remote_copy(
        src_ref=src,
        dst_ref=dst,
        send_sem=sent,
        recv_sem=landed,
        device_id=device,
        device_id_type=MESH,
    ).start()


def await_bytes(like, semaphore):
    pltpu.make_async_copy(like, like, semaphore).wait()


def split(value):
    high = value.astype(jnp.bfloat16)
    low = (value - high.astype(jnp.float32)).astype(jnp.bfloat16)
    return high, low


def dot(a, b):
    return jnp.dot(a, b, preferred_element_type=jnp.float32)


def dot_t(a, b):
    return lax.dot_general(a, b, (((1,), (1,)), ((), ())), preferred_element_type=jnp.float32)


def grafted(matrix, left_root, right_root):
    high, low = split(matrix)
    t_high, t_low = split(dot(left_root, high) + dot(left_root, low))
    shaped = dot(t_high, right_root) + dot(t_low, right_root)
    square_g = jnp.sum(matrix * matrix, keepdims=True) / matrix.size
    square_s = jnp.sum(shaped * shaped, keepdims=True) / matrix.size
    return shaped * (jnp.sqrt(square_g) / jnp.sqrt(square_s + EPS))


def half_grams(matrix):
    high, low = split(matrix)
    half = high * jnp.bfloat16(0.5)
    left = dot_t(high, half) + dot_t(high, low)
    high_t = high.T
    right = dot(high_t, half) + dot(high_t, low)
    return left, right


def pick(index, values):
    result = values[0]
    for k in range(1, len(values)):
        result = jnp.where(index == k, values[k], result)
    return result


def step_kernel(
    table_ref, grad_ref, stat_ref, root_ref, direction_ref, new_ref,
    near, mine, relay, coming, pieces, stage, blocks, roots, returning, far_out, near_out, far_in, merged,
    picked_row, picked,
    load_sem, sent_sem, relay_sent_sem, relay_sem, coming_sem, out_sent_sem, out_sem,
    back_sent_sem, back_sem, far_sent_sem, far_sem, merged_sent_sem, merged_sem, *came,
):
    place = Place()
    rows, half = mine.shape[0], mine.shape[1] // 2
    width = half // PARTS
    size = stage.shape[2]
    row_blocks, col_blocks = table_ref.shape

    def quarter(dy):
        return pl.ds(pl.multiple_of(place.ys[dy] * rows, rows), rows)

    def grad(dy, side, part=None):
        start, count = (side * half, half) if part is None else (side * half + part * width, width)
        return grad_ref.at[0, quarter(dy), pl.ds(start, count)]

    loads = [
        pltpu.make_async_copy(grad(1, 0), near.at[0], load_sem.at[0]),
        pltpu.make_async_copy(grad(3, 1), near.at[1], load_sem.at[1]),
        pltpu.make_async_copy(grad_ref.at[0, quarter(0)], mine, load_sem.at[2]),
    ]
    root_load = pltpu.make_async_copy(root_ref.at[0], roots, load_sem.at[3])
    stat_load = pltpu.make_async_copy(stat_ref, new_ref, load_sem.at[4])
    for load in loads:
        load.start()

    barrier = pltpu.get_barrier_semaphore()
    for dz, dx, dc, dy in ORDER:
        shard, y = place.in_plane(dx, dc, dy)
        device = (place.zs[dz] * SHARDS + shard, y)
        pl.semaphore_signal(barrier, inc=1, device_id=device, device_id_type=MESH)
    pl.semaphore_wait(barrier, len(ORDER))

    ways = ((1, 0), (3, 1))
    for part in range(PARTS):
        for to, side in ways:
            send(
                grad(2, side, part), relay.at[side, :, pl.ds(part * width, width)],
                sent_sem, relay_sem.at[side, part], place.line(to),
            )
    for part in range(PARTS):
        for to, side in ways:
            columns = pl.ds((1 - side) * half + part * width, width)
            send(
                grad(to, 1 - side, part), coming.at[side, :, columns],
                sent_sem, coming_sem.at[side, 1 - side, part], place.line(to),
            )

    lanes = lax.broadcasted_iota(jnp.int32, picked_row.shape, 1)
    columns_of = jnp.zeros(picked_row.shape, jnp.int32)
    for column in range(col_blocks):
        columns_of = jnp.where(lanes == table_ref[place.z, column], column, columns_of)
    picked_row[...] = columns_of
    picked_copy = pltpu.make_async_copy(picked_row, picked, load_sem.at[5])
    picked_copy.start()

    owned, slot_of_row = [], []
    total = jnp.int32(0)
    for row in range(row_blocks):
        count = jnp.int32(0)
        for column in range(col_blocks):
            count = jnp.where(table_ref[row, column] == place.index, 1, count)
        owned.append(count)
        slot_of_row.append(total)
        total += count
    row_of_slot = []
    for slot in range(row_blocks):
        row_of = jnp.int32(0)
        for row in range(row_blocks):
            row_of += jnp.where(slot_of_row[row] == slot, owned[row] * row, 0)
        row_of_slot.append(row_of)

    for load in loads:
        load.wait()
    for part in range(PARTS):
        for to, side in ways:
            here = pl.ds(part * width, width)
            block = relay.at[side, :, here]
            await_bytes(block, relay_sem.at[side, part])
            relay[side, :, here] += near[side, :, here]
            columns = pl.ds(side * half + part * width, width)
            send(
                block, coming.at[side, :, columns],
                relay_sent_sem, coming_sem.at[side, side, part], place.line(to),
            )
    root_load.start()
    stat_load.start()
    picked_copy.wait()
    for side in range(2):
        for part in range(PARTS):
            columns = pl.ds((1 - side) * half + part * width, width)
            await_bytes(coming.at[side, :, columns], coming_sem.at[side, 1 - side, part])
            mine[:, columns] += coming[side, :, columns]
    for part in range(PARTS):
        for side in range(2):
            start = side * half + part * width
            columns = pl.ds(start, width)
            await_bytes(coming.at[side, :, columns], coming_sem.at[side, side, part])
            for column in range(start, start + width, size):
                at = pl.ds(column, size)
                pieces[column // size] = mine[:, at] + coming[side, :, at]

    chunk = pl.ds(pl.multiple_of(place.chunk * rows, rows), rows)
    landing = blocks.at[place.z, chunk]
    for dz, dx, dc, dy in ORDER:
        shard, y = place.in_plane(dx, dc, dy)
        fsdp = place.zs[dz] * SHARDS + shard
        target = fsdp * RING + y
        stage[target] = pieces[picked[0, target]]
        send(stage.at[target], landing, out_sent_sem, out_sem.at[place.z], (fsdp, y))
    stage[place.index] = pieces[picked[0, place.index]]
    pltpu.make_async_copy(stage.at[place.index], landing, out_sem.at[place.z]).start()

    root_load.wait()
    shard_rows = rows * RING

    def rows_back(row, shard, part, remote=True):
        start = pl.multiple_of(shard * shard_rows + STARTS[part], 8)
        piece = returning.at[row, pl.ds(start, BACK[part])]
        landing = came[part].at[place.fsdp]
        if remote:
            send(piece, landing, back_sent_sem, back_sem.at[part], (row * SHARDS + shard, place.y))
        else:
            pltpu.make_async_copy(piece, landing, back_sem.at[part]).start()

    def two_rows(step, carry):
        planes = [jnp.where(step == 0, 2, 1), jnp.where(step == 0, 0, 3)]
        block_rows = [lax.rem(place.z + dz, RING) for dz in planes]
        for row in block_rows:
            await_bytes(blocks.at[row], out_sem.at[row])
            slot = pick(row, slot_of_row)
            returning[row] = grafted(blocks[row], roots[slot, 0], roots[slot, 1])
        for part in range(EARLY):
            for dz, dx, dc, _ in SAME_Y_ODD:
                row = block_rows[dz // 2]
                shard = place.in_plane(dx, dc, 0)[0]
                if dz == 1 or dx or dc:
                    rows_back(row, shard, part)
                else:
                    pl.when(step != 0)(functools.partial(rows_back, row, shard, part))
                    pl.when(step == 0)(functools.partial(rows_back, row, shard, part, False))
        return carry

    lax.fori_loop(0, row_blocks // 2, two_rows, 0)

    def all_rows_back(part):
        for dz, dx, dc, _ in SAME_Y:
            shard = place.in_plane(dx, dc, 0)[0]
            rows_back(place.zs[dz], shard, part, any((dz, dx, dc)))

    for part in range(EARLY, AHEAD):
        all_rows_back(part)

    per_quarter = direction_ref.shape[1] // size
    per_half = per_quarter // 2

    def columns_of_half(side):
        return [side * per_half + k for k in range(per_half)]

    def owner_of(dy, column):
        owner = table_ref[place.z, place.ys[dy] * per_quarter + column]
        return owner // RING, lax.rem(owner % RING - place.y + RING, RING)

    def here(part):
        return pl.ds(STARTS[part], BACK[part])

    def at(column):
        return pl.ds(column * size, size)

    half_width = per_half * size

    def send_own(part):
        await_bytes(came[part], back_sem.at[part])
        for side, to in ((0, 1), (1, 3)):
            for k, column in enumerate(columns_of_half(side)):
                far_out[side, here(part), at(k)] = came[part][owner_of(2, column)[0]]
            send(
                far_out.at[side, here(part)], far_in.at[side, here(part)],
                far_sent_sem, far_sem.at[side, part], place.line(to),
            )
        for side, to in ((0, 1), (1, 3)):
            other = pl.ds((1 - side) * half_width, half_width)
            for k, column in enumerate(columns_of_half(1 - side)):
                near_out[side, here(part), at(k)] = came[part][owner_of(to, column)[0]]
            send(
                near_out.at[side, here(part)], merged.at[side, here(part), other],
                far_sent_sem, merged_sem.at[side, 0, part], place.line(to),
            )

    def send_merged(part):
        for side, to in ((0, 1), (1, 3)):
            await_bytes(far_in.at[side, here(part)], far_sem.at[side, part])
            for k, column in enumerate(columns_of_half(side)):
                owner, relative = owner_of(to, column)
                own = came[part][owner]
                passed = far_in[side, here(part), at(k)]
                far_in[side, here(part), at(k)] = jnp.where(relative == (to + 2) % RING, passed, own)
            same = pl.ds(side * half_width, half_width)
            send(
                far_in.at[side, here(part)], merged.at[side, here(part), same],
                merged_sent_sem, merged_sem.at[side, 1, part], place.line(to),
            )

    def finish(part):
        for side in range(2):
            for kind in range(2):
                columns = pl.ds((side if kind else 1 - side) * half_width, half_width)
                await_bytes(merged.at[side, here(part), columns], merged_sem.at[side, kind, part])
        for column in range(per_quarter):
            owner, relative = owner_of(0, column)
            by_far = 0 if column < per_half else 1
            before = merged[0, here(part), at(column)]
            after = merged[1, here(part), at(column)]
            from_before = (relative == 3) | ((relative == 2) & (by_far == 0))
            passed = jnp.where(from_before, before, after)
            direction_ref[here(part), at(column)] = jnp.where(relative == 0, came[part][owner], passed)

    def renew(slot):
        left, right = half_grams(blocks[row_of_slot[slot]])
        live = slot < total
        for k, gram in enumerate((left, right)):
            renewed = BETA * new_ref[0, slot, k] + (1.0 - BETA) * (gram + gram.T)
            new_ref[0, slot, k] = jnp.where(live, renewed, 0.0)

    stat_load.wait()
    for part in range(len(BACK)):
        send_own(part)
        if part + AHEAD < len(BACK):
            all_rows_back(part + AHEAD)
        if part < row_blocks:
            renew(part)
        send_merged(part)
        if part:
            finish(part - 1)
    finish(len(BACK) - 1)

    await_bytes(mine, relay_sent_sem)
    await_bytes(coming, sent_sem)
    await_bytes(stage.at[pl.ds(0, len(ORDER))], out_sent_sem)
    await_bytes(stage.at[pl.ds(0, len(ORDER) + 1 - RING)], back_sent_sem)
    await_bytes(merged, far_sent_sem)
    await_bytes(far_in, merged_sent_sem)


def store_kernel(direction_ref, new_ref, direction_out, new_out, semaphore):
    copies = [pltpu.make_async_copy(direction_ref, direction_out, semaphore.at[0])]
    for slot in range(new_ref.shape[1]):
        copies.append(
            pltpu.make_async_copy(new_ref.at[0, slot], new_out.at[0, slot], semaphore.at[slot + 1])
        )
    for copy in copies:
        copy.start()
    for copy in copies:
        copy.wait()


def on_device(gradient, block_owner_table, statistics, inverse_fourth_roots):
    size = statistics.shape[3]
    row_blocks, col_blocks = block_owner_table.shape
    _, shard_rows, columns = gradient.shape
    rows = shard_rows // RING
    workers = RING * PLANE
    quarter = columns // RING
    dma = pltpu.SemaphoreType.DMA
    anywhere = pl.BlockSpec(memory_space=pl.ANY)
    direction, new_statistics = pl.pallas_call(
        step_kernel,
        out_shape=(
            pltpu.VMEM((shard_rows, quarter), jnp.float32),
            pltpu.VMEM(statistics.shape, jnp.float32),
        ),
        in_specs=[pl.BlockSpec(memory_space=pltpu.SMEM), anywhere, anywhere, anywhere],
        out_specs=(pl.BlockSpec(memory_space=pltpu.VMEM),) * 2,
        scratch_shapes=[
            pltpu.VMEM((2, rows, columns // 2), jnp.float32),
            pltpu.VMEM((rows, columns), jnp.float32),
            pltpu.VMEM((2, rows, columns // 2), jnp.float32),
            pltpu.VMEM((2, rows, columns), jnp.float32),
            pltpu.VMEM((col_blocks, rows, size), jnp.float32),
            pltpu.VMEM((workers, rows, size), jnp.float32),
            pltpu.VMEM((row_blocks, size, size), jnp.float32),
            pltpu.VMEM(inverse_fourth_roots.shape[1:], jnp.bfloat16),
            pltpu.VMEM((row_blocks, size, size), jnp.float32),
            pltpu.VMEM((2, shard_rows, quarter // 2), jnp.float32),
            pltpu.VMEM((2, shard_rows, quarter // 2), jnp.float32),
            pltpu.VMEM((2, shard_rows, quarter // 2), jnp.float32),
            pltpu.VMEM((2, shard_rows, quarter), jnp.float32),
            pltpu.VMEM((1, workers), jnp.int32),
            pltpu.SMEM((1, workers), jnp.int32),
            dma((6,)),
            dma,
            dma,
            dma((2, PARTS)),
            dma((2, 2, PARTS)),
            dma,
            dma((row_blocks,)),
            dma,
            dma((len(BACK),)),
            dma,
            dma((2, len(BACK))),
            dma,
            dma((2, 2, len(BACK))),
            *(pltpu.VMEM((workers // RING, part, size), jnp.float32) for part in BACK),
        ],
        compiler_params=pltpu.CompilerParams(
            collective_id=0, has_side_effects=True, vmem_limit_bytes=48 * 2**20
        ),
        name="shampoo_step",
    )(block_owner_table, gradient, statistics, inverse_fourth_roots)
    in_vmem = pl.BlockSpec(memory_space=pltpu.VMEM)
    return pl.pallas_call(
        store_kernel,
        out_shape=(
            jax.ShapeDtypeStruct(direction.shape, jnp.float32),
            jax.ShapeDtypeStruct(statistics.shape, jnp.float32),
        ),
        in_specs=[in_vmem, in_vmem],
        out_specs=(anywhere, anywhere),
        scratch_shapes=[dma((row_blocks + 1,))],
        compiler_params=pltpu.CompilerParams(vmem_limit_bytes=2**20),
        name="store",
    )(direction, new_statistics)


def solution(mesh):
    in_specs = (
        P("rep", "fsdp", None),
        P(),
        P(("fsdp", "rep"), None, None, None, None),
        P(("fsdp", "rep"), None, None, None, None),
    )
    out_specs = (P("fsdp", "rep"), P(("fsdp", "rep"), None, None, None, None))
    return jax.shard_map(
        on_device, mesh=mesh, in_specs=in_specs, out_specs=out_specs, check_vma=False
    )
```

```python
import functools
import itertools

import jax
import jax.numpy as jnp
from jax import lax
from jax.experimental import pallas as pl
from jax.experimental.pallas import tpu as pltpu
from jax.sharding import PartitionSpec as P

BETA = 0.9
EPS = 1e-06
MESH = pl.DeviceIdType.MESH
RING = 4
CORES = 2
SHARDS = RING * CORES
PLANE = SHARDS * RING
PARTS = 4
GATHERED = (8, 8, 8, 8)
BACK = (8, 8, 8, 8, 8, 8, 8, 8)
EARLY = 3
AHEAD = 3


def balanced(offsets):
    left, order, load = sorted(offsets), [], [0.0] * 6

    def hops(offset):
        dz, dx, _, dy = offset
        steps = []
        for d in (dz, dx, dy):
            steps += [1, 1] if d == 2 else [d == 1, d == 3]
        return steps

    while left:
        def cost(offset):
            after = [a + b for a, b in zip(load, hops(offset))]
            return (max(after) - sum(after) / 6, -sum(hops(offset)), offset)

        best = min(left, key=cost)
        left.remove(best)
        order.append(best)
        load = [a + b for a, b in zip(load, hops(best))]
    return order


def offsets(planes):
    every = itertools.product(planes, range(RING), range(CORES), range(RING))
    return [offset for offset in every if any(offset)]


ORDER = balanced(offsets((0, 2))) + balanced(offsets((1, 3)))
SAME_Y = balanced([offset for offset in offsets(range(RING)) if offset[3] == 0]) + [(0, 0, 0, 0)]
SAME_Y_ODD = [offset for offset in balanced(offsets((1, 3))) if offset[3] == 0]
STARTS = [sum(BACK[:k]) for k in range(len(BACK))]
WAYS = ((1, 0), (3, 1))


class Place:
    def __init__(self):
        fsdp, self.y = lax.axis_index("fsdp"), lax.axis_index("rep")
        self.fsdp = fsdp
        self.z = fsdp // SHARDS
        self.shard = fsdp % SHARDS
        self.chunk = self.shard * RING + self.y
        self.index = fsdp * RING + self.y
        x, c = self.shard // CORES, self.shard % CORES
        self.zs = [lax.rem(self.z + d, RING) for d in range(RING)]
        self.xs = [lax.rem(x + d, RING) * CORES for d in range(RING)]
        self.cs = [c, 1 - c]
        self.ys = [lax.rem(self.y + d, RING) for d in range(RING)]

    def in_plane(self, dx, dc, dy):
        shard = self.xs[dx] + self.cs[dc]
        return shard, self.ys[dy]

    def line(self, dy):
        return {"rep": self.ys[dy]}


def send(src, dst, sent, landed, device):
    pltpu.make_async_remote_copy(
        src_ref=src,
        dst_ref=dst,
        send_sem=sent,
        recv_sem=landed,
        device_id=device,
        device_id_type=MESH,
    ).start()


def await_bytes(like, semaphore):
    pltpu.make_async_copy(like, like, semaphore).wait()


def split(value):
    high = value.astype(jnp.bfloat16)
    low = (value - high.astype(jnp.float32)).astype(jnp.bfloat16)
    return high, low


def dot(a, b):
    return jnp.dot(a, b, preferred_element_type=jnp.float32)


def dot_t(a, b):
    return lax.dot_general(a, b, (((1,), (1,)), ((), ())), preferred_element_type=jnp.float32)


def grafted(matrix, left_root, right_root):
    high, low = split(matrix)
    t_high, t_low = split(dot(left_root, high) + dot(left_root, low))
    shaped = dot(t_high, right_root) + dot(t_low, right_root)
    square_g = jnp.sum(matrix * matrix, keepdims=True) / matrix.size
    square_s = jnp.sum(shaped * shaped, keepdims=True) / matrix.size
    return shaped * (jnp.sqrt(square_g) / jnp.sqrt(square_s + EPS))


def half_grams(matrix):
    high, low = split(matrix)
    half = high * jnp.bfloat16(0.5)
    left = dot_t(high, half) + dot_t(high, low)
    high_t = high.T
    right = dot(high_t, half) + dot(high_t, low)
    return left, right


def pick(index, values):
    result = values[0]
    for k in range(1, len(values)):
        result = jnp.where(index == k, values[k], result)
    return result


def step_kernel(
    table_ref, grad_ref, stat_ref, root_ref, direction_ref, new_ref,
    own, relay, coming, pieces, stage, top_relay, top_coming, top_stage,
    blocks, roots, returning, far_out, near_out, far_in, merged, picked_row, picked,
    load_sem, sent_sem, relay_sent_sem, relay_sem, coming_sem, out_sent_sem, out_sem,
    top_sent_sem, top_relay_sent_sem, top_relay_sem, top_coming_sem,
    gather_sent_sem, gather_sem, pass_sent_sem, pass_sem, top_out_sent_sem,
    back_sent_sem, back_sem, far_sent_sem, far_sem, merged_sent_sem, merged_sem, *lists,
):
    gathered, came = lists[: len(GATHERED)], lists[len(GATHERED) :]
    place = Place()
    shard_rows, all_columns = own.shape
    top_rows = sum(GATHERED)
    rows = (shard_rows - top_rows) // RING
    half = all_columns // 2
    width = half // PARTS
    quarter = all_columns // RING
    side_width = quarter // 2
    size = blocks.shape[2]
    row_blocks, col_blocks = table_ref.shape

    own_load = pltpu.make_async_copy(grad_ref.at[0], own, load_sem.at[0])
    root_load = pltpu.make_async_copy(root_ref.at[0], roots, load_sem.at[1])
    stat_load = pltpu.make_async_copy(stat_ref, new_ref, load_sem.at[2])
    own_load.start()

    barrier = pltpu.get_barrier_semaphore()
    for dz, dx, dc, dy in ORDER:
        shard, y = place.in_plane(dx, dc, dy)
        device = (place.zs[dz] * SHARDS + shard, y)
        pl.semaphore_signal(barrier, inc=1, device_id=device, device_id_type=MESH)
    pl.semaphore_wait(barrier, len(ORDER))

    per_quarter = quarter // size
    per_half = per_quarter // 2

    def at(column):
        return pl.ds(column * size, size)

    def top_here(part):
        return pl.ds(sum(GATHERED[:part]), GATHERED[part])

    def top_columns(dy, side=None):
        start = pl.multiple_of(place.ys[dy] * quarter, quarter)
        if side is None:
            return pl.ds(start, quarter)
        return pl.ds(pl.multiple_of(start + side * side_width, side_width), side_width)

    def top_blocks(dy, side):
        return pl.ds(place.ys[dy] * per_quarter + side * per_half, per_half)

    def side_of(side):
        return pl.ds(side * side_width, side_width)

    def top_send(part):
        here = top_here(part)
        for to, side in WAYS:
            send(
                grad_ref.at[0, here, top_columns(2, side)], top_relay.at[side, here],
                top_sent_sem, top_relay_sem.at[side, part], place.line(to),
            )
        for to, side in WAYS:
            send(
                grad_ref.at[0, here, top_columns(to, 1 - side)],
                top_coming.at[side, here, side_of(1 - side)],
                top_sent_sem, top_coming_sem.at[side, 0, part], place.line(to),
            )

    def top_pass(part):
        here = top_here(part)
        for to, side in WAYS:
            block = top_relay.at[side, here]
            await_bytes(block, top_relay_sem.at[side, part])
            top_relay[side, here] += own[here, top_columns(to, side)]
            send(
                block, top_coming.at[side, here, side_of(side)],
                top_relay_sent_sem, top_coming_sem.at[side, 1, part], place.line(to),
            )

    def top_gather(part):
        here = top_here(part)
        for side in range(2):
            for kind in range(2):
                columns = side_of(side if kind else 1 - side)
                await_bytes(top_coming.at[side, here, columns], top_coming_sem.at[side, kind, part])
        for k in range(per_quarter):
            start = pl.multiple_of(place.ys[0] * quarter + k * size, size)
            passed = top_coming[0, here, at(k)] + top_coming[1, here, at(k)]
            gathered[part][place.ys[0] * per_quarter + k] = own[here, pl.ds(start, size)] + passed
        for first in range(2):
            for to, side in WAYS:
                k = side if first == 0 else 1 - side
                block = gathered[part].at[top_blocks(0, k)]
                send(block, block, gather_sent_sem, gather_sem.at[side, k, part], place.line(to))

    def top_gather_on(part):
        for to, side in WAYS:
            block = gathered[part].at[top_blocks((to + 2) % RING, side)]
            await_bytes(block, gather_sem.at[side, side, part])
            send(block, block, pass_sent_sem, pass_sem.at[side, part], place.line(to))

    def top_dispatch(part):
        for side, dy in ((0, 3), (1, 1)):
            rest, far = gathered[part].at[top_blocks(dy, 1 - side)], gathered[part].at[top_blocks(2, side)]
            await_bytes(rest, gather_sem.at[side, 1 - side, part])
            await_bytes(far, pass_sem.at[side, part])
        start = pl.multiple_of(place.shard * shard_rows + sum(GATHERED[:part]), 8)
        landing = blocks.at[place.z, pl.ds(start, GATHERED[part])]
        for dz, dx, dc, _ in SAME_Y:
            fsdp = place.zs[dz] * SHARDS + place.in_plane(dx, dc, 0)[0]
            piece = top_stage.at[fsdp, top_here(part)]
            top_stage[fsdp, top_here(part)] = gathered[part][picked[0, fsdp * RING + place.y]]
            if any((dz, dx, dc)):
                send(piece, landing, top_out_sent_sem.at[part], out_sem.at[place.z], (fsdp, place.y))
            else:
                pltpu.make_async_copy(piece, landing, out_sem.at[place.z]).start()

    def low(dy):
        return pl.ds(pl.multiple_of(top_rows + place.ys[dy] * rows, 8), rows)

    def low_far(part):
        for to, side in WAYS:
            columns = pl.ds(side * half + part * width, width)
            send(
                grad_ref.at[0, low(2), columns], relay.at[side, :, pl.ds(part * width, width)],
                sent_sem, relay_sem.at[side, part], place.line(to),
            )

    def low_near(part):
        for to, side in WAYS:
            columns = pl.ds((1 - side) * half + part * width, width)
            send(
                grad_ref.at[0, low(to), columns], coming.at[side, :, columns],
                sent_sem, coming_sem.at[side, 0, part], place.line(to),
            )

    def low_pass(part):
        here = pl.ds(part * width, width)
        for to, side in WAYS:
            block = relay.at[side, :, here]
            await_bytes(block, relay_sem.at[side, part])
            columns = pl.ds(side * half + part * width, width)
            relay[side, :, here] += own[low(to), columns]
            send(
                block, coming.at[side, :, columns],
                relay_sent_sem, coming_sem.at[side, 1, part], place.line(to),
            )

    def low_finish(part):
        for side in range(2):
            start = side * half + part * width
            columns = pl.ds(start, width)
            await_bytes(coming.at[1 - side, :, columns], coming_sem.at[1 - side, 0, part])
            await_bytes(coming.at[side, :, columns], coming_sem.at[side, 1, part])
            for column in range(start, start + width, size):
                here = pl.ds(column, size)
                pieces[column // size] = own[low(0), here] + coming[0, :, here] + coming[1, :, here]

    top_send(0)
    top_send(1)

    lanes = lax.broadcasted_iota(jnp.int32, picked_row.shape, 1)
    columns_of = jnp.zeros(picked_row.shape, jnp.int32)
    for column in range(col_blocks):
        columns_of = jnp.where(lanes == table_ref[place.z, column], column, columns_of)
    picked_row[...] = columns_of
    picked_copy = pltpu.make_async_copy(picked_row, picked, load_sem.at[3])
    picked_copy.start()

    owned, slot_of_row = [], []
    total = jnp.int32(0)
    for row in range(row_blocks):
        count = jnp.int32(0)
        for column in range(col_blocks):
            count = jnp.where(table_ref[row, column] == place.index, 1, count)
        owned.append(count)
        slot_of_row.append(total)
        total += count
    row_of_slot = []
    for slot in range(row_blocks):
        row_of = jnp.int32(0)
        for row in range(row_blocks):
            row_of += jnp.where(slot_of_row[row] == slot, owned[row] * row, 0)
        row_of_slot.append(row_of)

    own_load.wait()
    root_load.start()
    stat_load.start()
    picked_copy.wait()
    top_pass(0)
    top_send(2)
    top_pass(1)
    top_gather(0)
    top_send(3)
    top_pass(2)
    top_gather(1)
    top_gather_on(0)
    top_pass(3)
    top_gather(2)
    top_gather_on(1)
    top_dispatch(0)
    top_gather(3)
    top_gather_on(2)
    top_dispatch(1)
    top_gather_on(3)
    for part in range(PARTS):
        low_far(part)
    for part in range(PARTS):
        low_near(part)
    top_dispatch(2)
    top_dispatch(3)
    for part in range(PARTS):
        low_pass(part)
    for part in range(PARTS):
        low_finish(part)

    start = pl.multiple_of(place.shard * shard_rows + top_rows + place.y * rows, 8)
    landing = blocks.at[place.z, pl.ds(start, rows)]
    for dz, dx, dc, dy in ORDER:
        shard, y = place.in_plane(dx, dc, dy)
        fsdp = place.zs[dz] * SHARDS + shard
        target = fsdp * RING + y
        stage[target] = pieces[picked[0, target]]
        send(stage.at[target], landing, out_sent_sem, out_sem.at[place.z], (fsdp, y))
    stage[place.index] = pieces[picked[0, place.index]]
    pltpu.make_async_copy(stage.at[place.index], landing, out_sem.at[place.z]).start()

    root_load.wait()

    def rows_back(row, shard, part, remote=True):
        start = pl.multiple_of(shard * shard_rows + STARTS[part], 8)
        piece = returning.at[row, pl.ds(start, BACK[part])]
        landing = came[part].at[place.fsdp]
        if remote:
            send(piece, landing, back_sent_sem.at[part], back_sem.at[part], (row * SHARDS + shard, place.y))
        else:
            pltpu.make_async_copy(piece, landing, back_sem.at[part]).start()

    def two_rows(step, carry):
        planes = [jnp.where(step == 0, 2, 1), jnp.where(step == 0, 0, 3)]
        block_rows = [lax.rem(place.z + dz, RING) for dz in planes]
        for row in block_rows:
            await_bytes(blocks.at[row], out_sem.at[row])
            slot = pick(row, slot_of_row)
            returning[row] = grafted(blocks[row], roots[slot, 0], roots[slot, 1])
        for part in range(EARLY):
            for dz, dx, dc, _ in SAME_Y_ODD:
                row = block_rows[dz // 2]
                shard = place.in_plane(dx, dc, 0)[0]
                if dz == 1 or dx or dc:
                    rows_back(row, shard, part)
                else:
                    pl.when(step != 0)(functools.partial(rows_back, row, shard, part))
                    pl.when(step == 0)(functools.partial(rows_back, row, shard, part, False))
        return carry

    lax.fori_loop(0, row_blocks // 2, two_rows, 0)

    def all_rows_back(part):
        for dz, dx, dc, _ in SAME_Y:
            shard = place.in_plane(dx, dc, 0)[0]
            rows_back(place.zs[dz], shard, part, any((dz, dx, dc)))

    for part in range(EARLY, AHEAD):
        all_rows_back(part)

    def columns_of_half(side):
        return [side * per_half + k for k in range(per_half)]

    def owner_of(dy, column):
        owner = table_ref[place.z, place.ys[dy] * per_quarter + column]
        return owner // RING, lax.rem(owner % RING - place.y + RING, RING)

    def here(part):
        return pl.ds(STARTS[part], BACK[part])

    half_width = per_half * size

    def send_own(part):
        await_bytes(came[part], back_sem.at[part])
        for side, to in ((0, 1), (1, 3)):
            for k, column in enumerate(columns_of_half(side)):
                far_out[side, here(part), at(k)] = came[part][owner_of(2, column)[0]]
            send(
                far_out.at[side, here(part)], far_in.at[side, here(part)],
                far_sent_sem, far_sem.at[side, part], place.line(to),
            )
        for side, to in ((0, 1), (1, 3)):
            other = pl.ds((1 - side) * half_width, half_width)
            for k, column in enumerate(columns_of_half(1 - side)):
                near_out[side, here(part), at(k)] = came[part][owner_of(to, column)[0]]
            send(
                near_out.at[side, here(part)], merged.at[side, here(part), other],
                far_sent_sem, merged_sem.at[side, 0, part], place.line(to),
            )

    def send_merged(part):
        for side, to in ((0, 1), (1, 3)):
            await_bytes(far_in.at[side, here(part)], far_sem.at[side, part])
            for k, column in enumerate(columns_of_half(side)):
                owner, relative = owner_of(to, column)
                own = came[part][owner]
                passed = far_in[side, here(part), at(k)]
                far_in[side, here(part), at(k)] = jnp.where(relative == (to + 2) % RING, passed, own)
            same = pl.ds(side * half_width, half_width)
            send(
                far_in.at[side, here(part)], merged.at[side, here(part), same],
                merged_sent_sem, merged_sem.at[side, 1, part], place.line(to),
            )

    def finish(part):
        for side in range(2):
            for kind in range(2):
                columns = pl.ds((side if kind else 1 - side) * half_width, half_width)
                await_bytes(merged.at[side, here(part), columns], merged_sem.at[side, kind, part])
        for column in range(per_quarter):
            owner, relative = owner_of(0, column)
            by_far = 0 if column < per_half else 1
            before = merged[0, here(part), at(column)]
            after = merged[1, here(part), at(column)]
            from_before = (relative == 3) | ((relative == 2) & (by_far == 0))
            passed = jnp.where(from_before, before, after)
            direction_ref[here(part), at(column)] = jnp.where(relative == 0, came[part][owner], passed)

    def renew(slot):
        left, right = half_grams(blocks[row_of_slot[slot]])
        live = slot < total
        for k, gram in enumerate((left, right)):
            renewed = BETA * new_ref[0, slot, k] + (1.0 - BETA) * (gram + gram.T)
            new_ref[0, slot, k] = jnp.where(live, renewed, 0.0)

    stat_load.wait()
    for part in range(len(BACK)):
        send_own(part)
        if part + AHEAD < len(BACK):
            all_rows_back(part + AHEAD)
        if part < row_blocks:
            renew(part)
        send_merged(part)
        if part:
            finish(part - 1)
    finish(len(BACK) - 1)

    await_bytes(coming, sent_sem)
    await_bytes(relay, relay_sent_sem)
    await_bytes(top_coming, top_sent_sem)
    await_bytes(top_relay, top_relay_sent_sem)
    await_bytes(top_coming, gather_sent_sem)
    await_bytes(top_relay, pass_sent_sem)
    await_bytes(stage.at[pl.ds(0, len(ORDER))], out_sent_sem)
    for part in range(len(GATHERED)):
        await_bytes(top_stage.at[pl.ds(0, len(SAME_Y) - 1), top_here(part)], top_out_sent_sem.at[part])
    for part in range(len(BACK)):
        await_bytes(came[part].at[pl.ds(0, len(SAME_Y) - 1)], back_sent_sem.at[part])
    await_bytes(merged, far_sent_sem)
    await_bytes(far_in, merged_sent_sem)


def store_kernel(direction_ref, new_ref, direction_out, new_out, semaphore):
    copies = [pltpu.make_async_copy(direction_ref, direction_out, semaphore.at[0])]
    for slot in range(new_ref.shape[1]):
        copies.append(
            pltpu.make_async_copy(new_ref.at[0, slot], new_out.at[0, slot], semaphore.at[slot + 1])
        )
    for copy in copies:
        copy.start()
    for copy in copies:
        copy.wait()


def on_device(gradient, block_owner_table, statistics, inverse_fourth_roots):
    size = statistics.shape[3]
    row_blocks, col_blocks = block_owner_table.shape
    _, shard_rows, columns = gradient.shape
    top_rows, tops = sum(GATHERED), len(GATHERED)
    rows = (shard_rows - top_rows) // RING
    workers = RING * PLANE
    quarter = columns // RING
    dma = pltpu.SemaphoreType.DMA
    anywhere = pl.BlockSpec(memory_space=pl.ANY)
    direction, new_statistics = pl.pallas_call(
        step_kernel,
        out_shape=(
            pltpu.VMEM((shard_rows, quarter), jnp.float32),
            pltpu.VMEM(statistics.shape, jnp.float32),
        ),
        in_specs=[pl.BlockSpec(memory_space=pltpu.SMEM), anywhere, anywhere, anywhere],
        out_specs=(pl.BlockSpec(memory_space=pltpu.VMEM),) * 2,
        scratch_shapes=[
            pltpu.VMEM((shard_rows, columns), jnp.float32),
            pltpu.VMEM((2, rows, columns // 2), jnp.float32),
            pltpu.VMEM((2, rows, columns), jnp.float32),
            pltpu.VMEM((col_blocks, rows, size), jnp.float32),
            pltpu.VMEM((workers, rows, size), jnp.float32),
            pltpu.VMEM((2, top_rows, quarter // 2), jnp.float32),
            pltpu.VMEM((2, top_rows, quarter), jnp.float32),
            pltpu.VMEM((workers // RING, top_rows, size), jnp.float32),
            pltpu.VMEM((row_blocks, size, size), jnp.float32),
            pltpu.VMEM(inverse_fourth_roots.shape[1:], jnp.bfloat16),
            pltpu.VMEM((row_blocks, size, size), jnp.float32),
            pltpu.VMEM((2, shard_rows, quarter // 2), jnp.float32),
            pltpu.VMEM((2, shard_rows, quarter // 2), jnp.float32),
            pltpu.VMEM((2, shard_rows, quarter // 2), jnp.float32),
            pltpu.VMEM((2, shard_rows, quarter), jnp.float32),
            pltpu.VMEM((1, workers), jnp.int32),
            pltpu.SMEM((1, workers), jnp.int32),
            dma((4,)),
            dma,
            dma,
            dma((2, PARTS)),
            dma((2, 2, PARTS)),
            dma,
            dma((row_blocks,)),
            dma,
            dma,
            dma((2, tops)),
            dma((2, 2, tops)),
            dma,
            dma((2, 2, tops)),
            dma,
            dma((2, tops)),
            dma((tops,)),
            dma((len(BACK),)),
            dma((len(BACK),)),
            dma,
            dma((2, len(BACK))),
            dma,
            dma((2, 2, len(BACK))),
            *(pltpu.VMEM((col_blocks, part, size), jnp.float32) for part in GATHERED),
            *(pltpu.VMEM((workers // RING, part, size), jnp.float32) for part in BACK),
        ],
        compiler_params=pltpu.CompilerParams(
            collective_id=0, has_side_effects=True, vmem_limit_bytes=48 * 2**20
        ),
        name="shampoo_step",
    )(block_owner_table, gradient, statistics, inverse_fourth_roots)
    in_vmem = pl.BlockSpec(memory_space=pltpu.VMEM)
    return pl.pallas_call(
        store_kernel,
        out_shape=(
            jax.ShapeDtypeStruct(direction.shape, jnp.float32),
            jax.ShapeDtypeStruct(statistics.shape, jnp.float32),
        ),
        in_specs=[in_vmem, in_vmem],
        out_specs=(anywhere, anywhere),
        scratch_shapes=[dma((row_blocks + 1,))],
        compiler_params=pltpu.CompilerParams(vmem_limit_bytes=2**20),
        name="store",
    )(direction, new_statistics)


def solution(mesh):
    in_specs = (
        P("rep", "fsdp", None),
        P(),
        P(("fsdp", "rep"), None, None, None, None),
        P(("fsdp", "rep"), None, None, None, None),
    )
    out_specs = (P("fsdp", "rep"), P(("fsdp", "rep"), None, None, None, None))
    return jax.shard_map(
        on_device, mesh=mesh, in_specs=in_specs, out_specs=out_specs, check_vma=False
    )
```
